256 devices in a mesh: gx: 8 (over z), gy: 16 (over x, y), ta: 2 (over core).
Axes of the slice: x: 4, y: 4, z: 8, core: 2. Of those that a mesh axis runs over, the one named last changes fastest.
Arguments:
- tokens: bfloat16 [32768, 1024], P(('gx', 'gy'), 'ta'), may hold values from -6 to 6
- cotangent: bfloat16 [32768, 1024], P(('gx', 'gy'), 'ta'), may hold values from -2 to 2
- gate_prob: bfloat16 [32768], P(('gx', 'gy')), may hold values from 0.049804688 to 1
- route_expert: int32 [32768], P(('gx', 'gy')), may hold values from 0 to 127
- route_slot: int32 [32768], P(('gx', 'gy')), may hold values from 0 to 2, as said below
- route_kept: int32 [32768], P(('gx', 'gy')), may hold values from 0 to 1, as said below
- w_in: bfloat16 [128, 1024, 2816], P(('gx', 'gy'), None, 'ta'), may hold values from -0.1875 to 0.1875
- w_out: bfloat16 [128, 2816, 1024], P(('gx', 'gy'), 'ta'), may hold values from -0.109375 to 0.109375
Outputs:
- grad_input: bfloat16 [32768, 1024], P(('gx', 'gy'), 'ta')
- gate_grad: bfloat16 [32768], P(('gx', 'gy'))
- grad_w_in: bfloat16 [128, 1024, 2816], P(('gx', 'gy'), None, 'ta')
- grad_w_out: bfloat16 [128, 2816, 1024], P(('gx', 'gy'), 'ta')
The draws below stay inside these ranges and needn't reach their ends.
Inputs may be any that keep to these rules, and one draw needn't show every extreme that they name: `route_slot`: among the kept tokens of one block that go to one expert, slots are distinct; a dropped token's slot is arbitrary. `route_kept`: at most 3 tokens of one block are kept for one expert; in every draw some expert has 3 kept tokens from every block.
All inputs are finite; a program needn't handle non-finite values.
Results may differ from the reference program's by a relative error of at most 0.0057.
Values may be sent and summed in bfloat16 or wider, within the bound.
A program may use at most 64 MiB of HBM per device.

```python
import math
import jax
import jax.numpy as jnp
from jax import lax

D = 1024
FF = 2816
TOK_DEV = 256
EXPERTS = 128
TOKENS = 32768
CAP = 3


def routing(key):
    block_count = TOKENS // TOK_DEV
    key_pop, key_pick, key_tail, key_uni, key_force, key_fill = jax.random.split(key, 6)
    popular = jax.random.permutation(key_pop, EXPERTS)[:4].astype(jnp.int32)
    chooser = jax.random.randint(key_pick, (TOKENS,), 0, 16)
    which_hot = jax.random.randint(key_tail, (TOKENS,), 0, 4)
    uniform_pick = jax.random.randint(key_uni, (TOKENS,), 0, EXPERTS)
    expert = jnp.where(chooser == 0, popular[which_hot], uniform_pick).astype(jnp.int32)

    def force_rank(block_key):
        return jax.random.permutation(block_key, TOK_DEV)
    force_keys = jax.random.split(key_force, block_count)
    ranks = jax.vmap(force_rank)(force_keys).reshape(TOKENS)
    expert = jnp.where(ranks < CAP, popular[0], expert).astype(jnp.int32)
    onehot = (expert.reshape(block_count, TOK_DEV)[:, :, None] == jnp.arange(EXPERTS, dtype=jnp.int32)[None, None, :]).astype(jnp.int32)
    prior = jnp.cumsum(onehot, axis=1) - onehot
    rank = jnp.sum(prior * onehot, axis=2).reshape(TOKENS)
    kept = (rank < CAP).astype(jnp.int32)
    filler = jax.random.randint(key_fill, (TOKENS,), 0, CAP)
    slot = jnp.where(kept == 1, rank, filler).astype(jnp.int32)
    return (expert, slot, kept)


def draw_route_expert(key, part):
    return routing(key)[0]


def draw_route_slot(key, part):
    return routing(key)[1]


def draw_route_kept(key, part):
    return routing(key)[2]


def level_of(own_key, dims, pieces, least, top_value):
    def one(axis_at, blocks):
        heights = jax.random.uniform(jax.random.fold_in(jax.random.fold_in(own_key, 6), axis_at), (blocks,), jnp.float32, least / len(pieces), top_value / len(pieces))
        return jnp.repeat(jnp.exp(heights), dims[axis_at] // blocks).reshape((-1,) + (1,) * (len(dims) - axis_at - 1))

    gain = one(*pieces[0])
    for cut in pieces[1:]:
        gain = gain * one(*cut)
    return gain


def centred(stream_key, extent, spread, bound, shards=(), kind=jnp.bfloat16):
    factor_of = level_of(stream_key, extent, shards, -0.22, 0.18) if shards else 1.0
    result = jax.random.normal(stream_key, extent, jnp.float32) * spread * factor_of
    return jnp.minimum(jnp.maximum(result, -bound), bound).astype(kind)


def setup_inputs(seed: int = 0) -> dict:
    keys = jax.random.split(jax.random.key(seed), 9)
    return {
        "tokens": centred(keys[0], (TOKENS, D), 1.0, 6.0, ((0, 128), (1, 2))),
        "cotangent": centred(keys[1], (TOKENS, D), 0.25, 2.0, ((0, 128), (1, 2))),
        "gate_prob": jnp.clip(jnp.exp(math.log(1.0) - 2.9996462 * jax.random.uniform(keys[2], (TOKENS,), jnp.float32) ** level_of(keys[2], (TOKENS,), ((0, 128),), -0.2, 0.2)), 0.049804688, 1.0).astype(jnp.bfloat16),
        "route_expert": draw_route_expert(jax.random.fold_in(keys[8], 71), 0),
        "route_slot": draw_route_slot(jax.random.fold_in(keys[8], 71), 0),
        "route_kept": draw_route_kept(jax.random.fold_in(keys[8], 71), 0),
        "w_in": centred(keys[6], (EXPERTS, D, FF), D ** -0.5, 0.1875, ((0, 128), (2, 2))),
        "w_out": centred(keys[7], (EXPERTS, FF, D), FF ** -0.5, 0.109375, ((0, 128), (1, 2))),
    }


tanh_scale = 0.7978845608
cubic_term = 0.044715


def gelu_value(value):
    return 0.5 * value * (1.0 + jnp.tanh(tanh_scale * (value + cubic_term * value * value * value)))


def gelu_slope(value):
    bent = jnp.tanh(tanh_scale * (value + cubic_term * value * value * value))
    return 0.5 * (1.0 + bent) + 0.5 * value * (1.0 - bent * bent) * tanh_scale * (1.0 + 3.0 * cubic_term * value * value)


def expert_grads(slot_tokens, slot_cotangent, slot_gate, w_first, w_second):
    pre_act = jnp.dot(slot_tokens, w_first, preferred_element_type=jnp.float32)
    hidden = gelu_value(pre_act).astype(jnp.bfloat16)
    expert_out = jnp.dot(hidden, w_second, preferred_element_type=jnp.float32)
    gate_part = jnp.sum(slot_cotangent.astype(jnp.float32) * expert_out, axis=1)
    scaled = (slot_gate.astype(jnp.float32)[:, None] * slot_cotangent.astype(jnp.float32)).astype(jnp.bfloat16)
    grad_second = jnp.dot(hidden.T, scaled, preferred_element_type=jnp.float32)
    grad_hidden = jnp.dot(scaled, w_second.T, preferred_element_type=jnp.float32)
    grad_pre = (grad_hidden * gelu_slope(pre_act)).astype(jnp.bfloat16)
    grad_first = jnp.dot(slot_tokens.T, grad_pre, preferred_element_type=jnp.float32)
    grad_tokens = jnp.dot(grad_pre, w_first.T, preferred_element_type=jnp.float32)
    return grad_first, grad_second, grad_tokens, gate_part


def reference(tokens, cotangent, gate_prob, route_expert, route_slot, route_kept, w_in, w_out):
    block_count = TOKENS // TOK_DEV
    slot_total = EXPERTS * block_count * CAP
    position = jnp.arange(TOKENS, dtype=jnp.int32)
    source_block = position // TOK_DEV
    is_kept = route_kept == 1
    flat_dest = jnp.where(is_kept, route_expert * (block_count * CAP) + source_block * CAP + route_slot, slot_total).astype(jnp.int32)
    slot_table = jnp.full((slot_total,), TOKENS, jnp.int32).at[flat_dest].set(position, mode="drop")
    slot_table = slot_table.reshape(EXPERTS, block_count * CAP)
    tokens_pad = jnp.concatenate([tokens, jnp.zeros((1, D), jnp.bfloat16)], axis=0)
    cotangent_pad = jnp.concatenate([cotangent, jnp.zeros((1, D), jnp.bfloat16)], axis=0)
    gate_pad = jnp.concatenate([gate_prob, jnp.zeros((1,), jnp.bfloat16)], axis=0)

    def one_expert(inputs):
        slot_index, w_first, w_second = inputs
        grad_first, grad_second, grad_tokens, gate_part = expert_grads(
            tokens_pad[slot_index], cotangent_pad[slot_index], gate_pad[slot_index], w_first, w_second)
        return (grad_first.astype(jnp.bfloat16), grad_second.astype(jnp.bfloat16),
                grad_tokens.astype(jnp.bfloat16), gate_part.astype(jnp.bfloat16))

    grad_w_in, grad_w_out, grad_slots, gate_slots = lax.map(one_expert, (slot_table, w_in, w_out))
    safe_dest = jnp.minimum(flat_dest, slot_total - 1).astype(jnp.int32)
    grad_rows = grad_slots.reshape(slot_total, D)[safe_dest]
    grad_input = jnp.where(is_kept[:, None], grad_rows, jnp.zeros_like(grad_rows))
    gate_rows = gate_slots.reshape(slot_total)[safe_dest]
    gate_grad = jnp.where(is_kept, gate_rows, jnp.zeros_like(gate_rows))
    return grad_input, gate_grad, grad_w_in, grad_w_out
```

```python
import functools

import jax
import jax.numpy as jnp
from jax import lax
from jax.experimental import pallas as pl
from jax.experimental.pallas import tpu as pltpu
from jax.sharding import PartitionSpec as P

MESH = pl.DeviceIdType.MESH
F32 = jnp.float32
BF16 = jnp.bfloat16

tanh_scale = 0.7978845608
cubic_term = 0.044715

PEERS = 128
CAP = 3
CHUNKS = 2
KC = PEERS // CHUNKS
RC = KC * CAP
ROWS = PEERS * CAP
TOK = 256
D = 1024
HALF = 512
FF = 1408
LB = HALF // 128
OUT_R = 2 * CAP * LB
BACK_R = 16
FT = [(i, min(256, FF - i)) for i in range(0, FF, 256)]

NN = (((1,), (0,)), ((), ()))
NT = (((1,), (1,)), ((), ()))
TN = (((0,), (0,)), ((), ()))


def dot(a, b, dims):
    return lax.dot_general(a, b, dims, preferred_element_type=F32)


def coords():
    g = lax.axis_index("gy")
    return lax.axis_index("gx"), g // 4, g % 4, lax.axis_index("ta")


def peer(k, sign):
    z, x, y, c = coords()
    dy, dx, dz = k // 32, (k // 8) % 4, k % 8
    return (
        (z + sign * dz + 8) % 8,
        ((x + sign * dx + 4) % 4) * 4 + (y + sign * dy + 4) % 4,
        c,
    )


def await_bytes(ref, sem):
    pltpu.make_async_copy(ref, ref, sem).wait()


def kernel(
    tok_hbm, cot_hbm, gate_ref, exp_ref, slot_ref, kept_ref, w1_hbm, w2_hbm,
    gin_ref, ggate_ref, gw1_hbm, gw2_hbm,
    tok, cot, w1, w2, pick, stage, stage_b, sbuf, rbuf, xs, hid, gp,
    part_s, part_r, bsend, brecv, grows, gw1, gw2,
    in_sem, w_sem, out_send, out_recv, back_send, back_recv, sib_send, sib_recv, wb_sem,
):
    z, x, y, c = coords()
    tok_in = pltpu.make_async_copy(tok_hbm, tok, in_sem.at[0])
    cot_in = pltpu.make_async_copy(cot_hbm, cot, in_sem.at[1])
    w1_in = pltpu.make_async_copy(w1_hbm, w1, w_sem.at[0])
    w2_in = pltpu.make_async_copy(w2_hbm, w2, w_sem.at[1])
    tok_in.start()
    cot_in.start()

    barrier = pltpu.get_barrier_semaphore()

    def greet(k, carry):
        pl.semaphore_signal(barrier, 1, device_id=peer(k, 1), device_id_type=MESH)
        return carry

    lax.fori_loop(1, PEERS, greet, 0)
    pl.semaphore_signal(barrier, 1, device_id={"ta": 1 - c}, device_id_type=MESH)
    w1_in.start()
    w2_in.start()

    expert = exp_ref[...]
    dz = ((expert >> 4) - z) & 7
    dx = (((expert >> 2) & 3) - x) & 3
    dy = ((expert & 3) - y) & 3
    k_tok = dy * 32 + dx * 8 + dz
    row_tok = (k_tok // KC) * RC + slot_ref[...] * KC + k_tok % KC
    row_tok = jnp.where(kept_ref[...] == 1, row_tok, -1)
    gate = gate_ref[...].astype(F32)
    tok_in.wait()
    cot_in.wait()

    def build(h):
        hot = lax.broadcasted_iota(jnp.int32, (RC, TOK), 0) + h * RC == row_tok
        sel = jnp.where(hot, 1.0, 0.0).astype(BF16)
        pick[pl.ds(h * RC, RC), :] = sel
        sel_gate = jnp.where(hot, gate, 0.0).astype(BF16)
        for a, (m, src) in enumerate(((sel, tok), (sel_gate, cot))):
            rows = dot(m, src[...], NN)
            for s in range(CAP):
                for j in range(LB):
                    stage[pl.ds((a * CAP + s) * LB + j, KC, stride=OUT_R), :] = rows[
                        s * KC : (s + 1) * KC, j * 128 : (j + 1) * 128
                    ]
        sbuf[pl.ds(h * KC, KC)] = stage[...].reshape(KC, OUT_R, 128).astype(BF16)

    def exchange(src, dst, ss, rs, sign, h):
        def one(k, carry):
            pltpu.make_async_remote_copy(
                src_ref=src.at[k], dst_ref=dst.at[k], send_sem=ss, recv_sem=rs,
                device_id=peer(k, sign), device_id_type=MESH,
            ).start()
            return carry

        lax.fori_loop(max(1, h * KC), (h + 1) * KC, one, 0)

    def arrived(ref, sem, h):
        lo = max(1, h * KC)
        await_bytes(ref.at[pl.ds(lo, (h + 1) * KC - lo)], sem)

    build(0)
    pl.semaphore_wait(barrier, PEERS)
    exchange(sbuf, rbuf, out_send.at[0], out_recv.at[0], 1, 0)
    rbuf[0] = sbuf[0]
    for h in range(1, CHUNKS):
        build(h)
        exchange(sbuf, rbuf, out_send.at[h], out_recv.at[h], 1, h)

    stage_b[...] = jnp.zeros_like(stage_b)
    w1_in.wait()
    w2_in.wait()

    def sibling(src, dst, sem):
        return pltpu.make_async_remote_copy(
            src_ref=src, dst_ref=dst, send_sem=sib_send.at[sem], recv_sem=sib_recv.at[sem],
            device_id={"ta": 1 - c}, device_id_type=MESH,
        )

    for h in range(CHUNKS):
        r0 = h * RC
        rr = pl.ds(r0, RC)
        arrived(rbuf, out_recv.at[h], h)
        stage[...] = rbuf[pl.ds(h * KC, KC)].astype(F32).reshape(KC * OUT_R, 128)
        for a in range(2):
            for s in range(CAP):
                for j in range(LB):
                    xs[c, a, r0 + s * KC : r0 + (s + 1) * KC, j * 128 : (j + 1) * 128] = stage[
                        pl.ds((a * CAP + s) * LB + j, KC, stride=OUT_R), :
                    ].astype(BF16)
        share = sibling(xs.at[c, :, rr], xs.at[c, :, rr], 2 * h)
        share.start()
        share.wait()

        gates = jnp.zeros((RC, 1), F32)
        for f0, fn in FT:
            pre = dot(xs[0, 0, rr], w1[0:HALF, f0 : f0 + fn], NN) + dot(
                xs[1, 0, rr], w1[HALF:D, f0 : f0 + fn], NN
            )
            up = dot(xs[0, 1, rr], w2[f0 : f0 + fn, 0:HALF], NT) + dot(
                xs[1, 1, rr], w2[f0 : f0 + fn, HALF:D], NT
            )
            sq = pre * pre
            th = jnp.tanh(tanh_scale * (pre + cubic_term * pre * sq))
            half = 0.5 * (1.0 + th)
            hb = (pre * half).astype(BF16)
            hid[rr, f0 : f0 + fn] = hb
            gates += jnp.sum(hb.astype(F32) * up, axis=1, keepdims=True)
            slope = half + 0.5 * pre * (1.0 - th * th) * tanh_scale * (1.0 + 3.0 * cubic_term * sq)
            gp[rr, f0 : f0 + fn] = (up * slope).astype(BF16)

        other = pl.multiple_of((1 - c) * HALF, HALF)
        mine = pl.multiple_of(c * HALF, HALF)
        gates = jnp.broadcast_to(gates, (RC, 128))
        part_s[h, :, 0:HALF] = dot(gp[rr, :], w1[pl.ds(other, HALF), :], NT)
        part_s[h, :, HALF : HALF + 128] = gates
        part = sibling(part_s.at[h], part_r.at[h], 2 * h + 1)
        part.start()
        own = dot(gp[rr, :], w1[pl.ds(mine, HALF), :], NT)
        part.wait()
        own = own + part_r[h, :, 0:HALF]
        gates = gates + part_r[h, :, HALF : HALF + 128]
        high = gates.astype(BF16).astype(F32)
        gates = jnp.where(
            lax.broadcasted_iota(jnp.int32, (RC, 128), 1) < 64, high, gates - high
        )
        for s in range(CAP):
            for j in range(LB):
                stage_b[pl.ds(s * LB + j, KC, stride=BACK_R), :] = own[
                    s * KC : (s + 1) * KC, j * 128 : (j + 1) * 128
                ]
            stage_b[pl.ds(CAP * LB + s, KC, stride=BACK_R), :] = gates[s * KC : (s + 1) * KC]
        bsend[pl.ds(h * KC, KC)] = stage_b[...].reshape(KC, BACK_R, 128).astype(BF16)
        exchange(bsend, brecv, back_send.at[h], back_recv.at[h], -1, h)
        if h == 0:
            brecv[0] = bsend[0]

    for i, (f0, fn) in enumerate(FT):
        for q in range(2):
            gw2[f0 : f0 + fn, q * HALF : (q + 1) * HALF] = dot(
                hid[:, f0 : f0 + fn], xs[q, 1], TN
            ).astype(BF16)
    gw2_out = pltpu.make_async_copy(gw2, gw2_hbm, wb_sem.at[0])
    gw2_out.start()
    for q in range(2):
        for d0 in range(0, HALF, 256):
            gw1[q * HALF + d0 : q * HALF + d0 + 256, :] = dot(
                xs[q, 0, :, d0 : d0 + 256], gp[...], TN
            ).astype(BF16)
    gw1_out = pltpu.make_async_copy(gw1, gw1_hbm, wb_sem.at[1])
    gw1_out.start()

    total = jnp.zeros((1, TOK), F32)
    for h in range(CHUNKS):
        arrived(brecv, back_recv.at[h], h)
        stage_b[...] = brecv[pl.ds(h * KC, KC)].astype(F32).reshape(KC * BACK_R, 128)
        for s in range(CAP):
            r0 = h * RC + s * KC
            for j in range(LB):
                grows[r0 : r0 + KC, j * 128 : (j + 1) * 128] = stage_b[
                    pl.ds(s * LB + j, KC, stride=BACK_R), :
                ].astype(BF16)
            both = stage_b[pl.ds(CAP * LB + s, KC, stride=BACK_R), :]
            value = both[:, 0:1] + both[:, 64:65]
            total += jnp.sum(
                pick[r0 : r0 + KC, :].astype(F32) * value, axis=0, keepdims=True
            )
    gin_ref[...] = dot(pick[...], grows[...], TN).astype(BF16)
    ggate_ref[...] = (total / gate).astype(BF16)

    for h in range(CHUNKS):
        arrived(sbuf, out_send.at[h], h)
        arrived(bsend, back_send.at[h], h)
    gw2_out.wait()
    gw1_out.wait()


def body(tokens, cotangent, gate_prob, route_expert, route_slot, route_kept, w_in, w_out):
    vmem = pl.BlockSpec(memory_space=pltpu.VMEM)
    hbm = pl.BlockSpec(memory_space=pl.ANY)
    dma = pltpu.SemaphoreType.DMA
    gin, ggate, gw1, gw2 = pl.pallas_call(
        kernel,
        out_shape=(
            jax.ShapeDtypeStruct((TOK, HALF), BF16),
            jax.ShapeDtypeStruct((1, TOK), BF16),
            jax.ShapeDtypeStruct((D, FF), BF16),
            jax.ShapeDtypeStruct((FF, D), BF16),
        ),
        in_specs=[hbm, hbm, vmem, vmem, vmem, vmem, hbm, hbm],
        out_specs=(vmem, vmem, hbm, hbm),
        scratch_shapes=[
            pltpu.VMEM((TOK, HALF), BF16),
            pltpu.VMEM((TOK, HALF), BF16),
            pltpu.VMEM((D, FF), BF16),
            pltpu.VMEM((FF, D), BF16),
            pltpu.VMEM((ROWS, TOK), BF16),
            pltpu.VMEM((KC * OUT_R, 128), F32),
            pltpu.VMEM((KC * BACK_R, 128), F32),
            pltpu.VMEM((PEERS, OUT_R, 128), BF16),
            pltpu.VMEM((PEERS, OUT_R, 128), BF16),
            pltpu.VMEM((2, 2, ROWS, HALF), BF16),
            pltpu.VMEM((ROWS, FF), BF16),
            pltpu.VMEM((ROWS, FF), BF16),
            pltpu.VMEM((CHUNKS, RC, HALF + 128), F32),
            pltpu.VMEM((CHUNKS, RC, HALF + 128), F32),
            pltpu.VMEM((PEERS, BACK_R, 128), BF16),
            pltpu.VMEM((PEERS, BACK_R, 128), BF16),
            pltpu.VMEM((ROWS, HALF), BF16),
            pltpu.VMEM((D, FF), BF16),
            pltpu.VMEM((FF, D), BF16),
            dma((2,)),
            dma((2,)),
            dma((CHUNKS,)),
            dma((CHUNKS,)),
            dma((CHUNKS,)),
            dma((CHUNKS,)),
            dma((2 * CHUNKS,)),
            dma((2 * CHUNKS,)),
            dma((2,)),
        ],
        compiler_params=pltpu.CompilerParams(
            collective_id=0, has_side_effects=True, vmem_limit_bytes=56 << 20
        ),
    )(
        tokens,
        cotangent,
        gate_prob.reshape(1, TOK),
        route_expert.reshape(1, TOK),
        route_slot.reshape(1, TOK),
        route_kept.reshape(1, TOK),
        w_in[0],
        w_out[0],
    )
    return gin, ggate.reshape(TOK), gw1[None], gw2[None]


def solution(mesh):
    placed = (
        P(("gx", "gy"), "ta"),
        P(("gx", "gy"), "ta"),
        P(("gx", "gy")),
        P(("gx", "gy")),
        P(("gx", "gy")),
        P(("gx", "gy")),
        P(("gx", "gy"), None, "ta"),
        P(("gx", "gy"), "ta", None),
    )
    return jax.shard_map(
        body,
        mesh=mesh,
        in_specs=placed,
        out_specs=(
            P(("gx", "gy"), "ta"),
            P(("gx", "gy")),
            P(("gx", "gy"), None, "ta"),
            P(("gx", "gy"), "ta", None),
        ),
        check_vma=False,
    )
```

```python
import functools

import jax
import jax.numpy as jnp
from jax import lax
from jax.experimental import pallas as pl
from jax.experimental.pallas import tpu as pltpu
from jax.sharding import PartitionSpec as P

MESH = pl.DeviceIdType.MESH
F32 = jnp.float32
BF16 = jnp.bfloat16

tanh_scale = 0.7978845608
cubic_term = 0.044715

PEERS = 128
CAP = 3
SIZES = (64, 48, 16)
STARTS = tuple(sum(SIZES[:i]) for i in range(len(SIZES)))
CHUNKS = len(SIZES)
BIG = max(SIZES)
ROWS = PEERS * CAP
TOK = 256
D = 1024
HALF = 512
FF = 1408
LB = HALF // 128
OUT_R = 2 * CAP * LB
BACK_R = 16
FT = [(i, min(256, FF - i)) for i in range(0, FF, 256)]

NN = (((1,), (0,)), ((), ()))
NT = (((1,), (1,)), ((), ()))
TN = (((0,), (0,)), ((), ()))


def dot(a, b, dims):
    return lax.dot_general(a, b, dims, preferred_element_type=F32)


def coords():
    g = lax.axis_index("gy")
    return lax.axis_index("gx"), g // 4, g % 4, lax.axis_index("ta")


def await_bytes(ref, sem):
    pltpu.make_async_copy(ref, ref, sem).wait()


def kernel(
    tok_hbm, cot_hbm, gate_hbm, exp_hbm, slot_hbm, kept_hbm, w1_hbm, w2_hbm,
    gw1, gw2, pick, grows, ggate_ref,
    tok, cot, gate_ref, exp_ref, slot_ref, kept_ref, w1, w2, stage, stage_b, sbuf, rbuf, xs, hid, gp, pre_acc, up_acc,
    part_s, part_r, bsend, brecv,
    in_sem, w_sem, out_send, out_recv, back_send, back_recv, sib_send, sib_recv, plane_sem,
):
    z, x, y, c = coords()
    zs = [lax.rem(z + d, 8) for d in range(8)]
    pairs = (
        (exp_hbm, exp_ref), (slot_hbm, slot_ref), (kept_hbm, kept_ref), (gate_hbm, gate_ref),
        (tok_hbm, tok), (cot_hbm, cot),
    )
    inputs = [pltpu.make_async_copy(src, dst, in_sem.at[i]) for i, (src, dst) in enumerate(pairs)]
    for copy in inputs:
        copy.start()
    weights = []
    for q in range(2):
        cols = pl.ds(q * HALF, HALF)
        weights.append(pltpu.make_async_copy(w1_hbm.at[cols], w1.at[q], w_sem.at[2 * q]))
        weights.append(pltpu.make_async_copy(w2_hbm.at[:, cols], w2.at[q], w_sem.at[2 * q + 1]))

    barrier = pltpu.get_barrier_semaphore()

    def ring(sem):
        for d in range(1, 8):
            pl.semaphore_signal(sem, 1, device_id={"gx": zs[d]}, device_id_type=MESH)

    ring(barrier)
    for d in range(1, 16):
        pl.semaphore_signal(barrier, 1, device_id={"gy": (x * 4 + y + d) % 16}, device_id_type=MESH)
    pl.semaphore_signal(barrier, 1, device_id={"ta": 1 - c}, device_id_type=MESH)
    for copy in weights:
        copy.start()
    for copy in inputs:
        copy.wait()

    expert = exp_ref[...]
    dz = ((expert >> 4) - z) & 7
    dx = (((expert >> 2) & 3) - x) & 3
    dy = ((expert & 3) - y) & 3
    k_tok = dy * 32 + dx * 8 + dz
    row_tok = CAP * STARTS[0] + slot_ref[...] * SIZES[0] + k_tok - STARTS[0]
    for k0, kc in zip(STARTS[1:], SIZES[1:]):
        row_tok = jnp.where(k_tok >= k0, CAP * k0 + slot_ref[...] * kc + k_tok - k0, row_tok)
    row_tok = jnp.where(kept_ref[...] == 1, row_tok, -1)
    gate = gate_ref[...].astype(F32).reshape(1, TOK)

    def build(h):
        k0, kc = STARTS[h], SIZES[h]
        rr = pl.ds(CAP * k0, CAP * kc)
        hot = lax.broadcasted_iota(jnp.int32, (CAP * kc, TOK), 0) + CAP * k0 == row_tok
        sel = jnp.where(hot, 1.0, 0.0).astype(BF16)
        pick[rr, :] = sel
        sel_gate = jnp.where(hot, gate, 0.0).astype(BF16)
        for a, (m, src) in enumerate(((sel, tok), (sel_gate, cot))):
            rows = dot(m, src[...], NN)
            for s in range(CAP):
                for j in range(LB):
                    stage[pl.ds((a * CAP + s) * LB + j, kc, stride=OUT_R), :] = rows[
                        s * kc : (s + 1) * kc, j * 128 : (j + 1) * 128
                    ]
        sbuf[pl.ds(k0, kc)] = stage[0 : kc * OUT_R].reshape(kc, OUT_R, 128).astype(BF16)

    def exchange(src, dst, ss, rs, sign, h):
        def group(g, lo):
            gx_at = [zs[(sign * d) % 8] for d in range(8)]
            dy, dx = g // 4, g % 4
            gy_at = lax.rem(x + sign * dx + 4, 4) * 4 + lax.rem(y + sign * dy + 4, 4)
            for d in range(lo, 8):
                pltpu.make_async_remote_copy(
                    src_ref=src.at[g * 8 + d], dst_ref=dst.at[g * 8 + d], send_sem=ss, recv_sem=rs,
                    device_id=(gx_at[d], gy_at, c), device_id_type=MESH,
                ).start()

        first = STARTS[h] // 8
        if first == 0:
            group(0, 1)
            first = 1

        def rest(g, carry):
            group(g, 0)
            return carry

        lax.fori_loop(first, (STARTS[h] + SIZES[h]) // 8, rest, 0)

    def arrived(ref, sem, h):
        lo = max(1, STARTS[h])
        await_bytes(ref.at[pl.ds(lo, STARTS[h] + SIZES[h] - lo)], sem)

    build(0)
    pl.semaphore_wait(barrier, 23)
    ring(plane_sem)
    pl.semaphore_wait(plane_sem, 7)
    exchange(sbuf, rbuf, out_send.at[0], out_recv.at[0], 1, 0)
    rbuf[0] = sbuf[0]
    for h in range(1, CHUNKS):
        build(h)
        exchange(sbuf, rbuf, out_send.at[h], out_recv.at[h], 1, h)

    stage_b[...] = jnp.zeros_like(stage_b)
    for copy in weights:
        copy.wait()

    def sibling(src, dst, sem):
        return pltpu.make_async_remote_copy(
            src_ref=src, dst_ref=dst, send_sem=sib_send.at[sem], recv_sem=sib_recv.at[sem],
            device_id={"ta": 1 - c}, device_id_type=MESH,
        )

    for h in range(CHUNKS):
        k0, kc = STARTS[h], SIZES[h]
        r0, rc = CAP * k0, CAP * kc
        rr = pl.ds(r0, rc)
        arrived(rbuf, out_recv.at[h], h)
        stage[0 : kc * OUT_R] = rbuf[pl.ds(k0, kc)].astype(F32).reshape(kc * OUT_R, 128)
        for a in range(2):
            for s in range(CAP):
                for j in range(LB):
                    xs[c, a, r0 + s * kc : r0 + (s + 1) * kc, j * 128 : (j + 1) * 128] = stage[
                        pl.ds((a * CAP + s) * LB + j, kc, stride=OUT_R), :
                    ].astype(BF16)
        share = sibling(xs.at[c, :, rr], xs.at[c, :, rr], 2 * h)
        share.start()
        for f0, fn in FT:
            pre_acc[0:rc, f0 : f0 + fn] = dot(xs[c, 0, rr], w1[c, :, f0 : f0 + fn], NN)
            up_acc[0:rc, f0 : f0 + fn] = dot(xs[c, 1, rr], w2[c, f0 : f0 + fn, :], NT)
        share.wait()

        gates = jnp.zeros((rc, 1), F32)
        for f0, fn in FT:
            pre = pre_acc[0:rc, f0 : f0 + fn] + dot(xs[1 - c, 0, rr], w1[1 - c, :, f0 : f0 + fn], NN)
            up = up_acc[0:rc, f0 : f0 + fn] + dot(xs[1 - c, 1, rr], w2[1 - c, f0 : f0 + fn, :], NT)
            sq = pre * pre
            th = jnp.tanh(tanh_scale * (pre + cubic_term * pre * sq))
            half = 0.5 * (1.0 + th)
            hb = (pre * half).astype(BF16)
            hid[rr, f0 : f0 + fn] = hb
            gates += jnp.sum(hb.astype(F32) * up, axis=1, keepdims=True)
            slope = half + 0.5 * pre * (1.0 - th * th) * tanh_scale * (1.0 + 3.0 * cubic_term * sq)
            gp[rr, f0 : f0 + fn] = (up * slope).astype(BF16)

        gates = jnp.broadcast_to(gates, (rc, 128))
        part_s[rr, 0:HALF] = dot(gp[rr, :], w1[1 - c], NT)
        part_s[rr, HALF : HALF + 128] = gates
        part = sibling(part_s.at[rr], part_r.at[rr], 2 * h + 1)
        part.start()
        own = dot(gp[rr, :], w1[c], NT)
        part.wait()
        own = own + part_r[rr, 0:HALF]
        gates = gates + part_r[rr, HALF : HALF + 128]
        high = gates.astype(BF16).astype(F32)
        gates = jnp.where(
            lax.broadcasted_iota(jnp.int32, (rc, 128), 1) < 64, high, gates - high
        )
        for s in range(CAP):
            for j in range(LB):
                stage_b[pl.ds(s * LB + j, kc, stride=BACK_R), :] = own[
                    s * kc : (s + 1) * kc, j * 128 : (j + 1) * 128
                ]
            stage_b[pl.ds(CAP * LB + s, kc, stride=BACK_R), :] = gates[s * kc : (s + 1) * kc]
        bsend[pl.ds(k0, kc)] = stage_b[0 : kc * BACK_R].reshape(kc, BACK_R, 128).astype(BF16)
        exchange(bsend, brecv, back_send.at[h], back_recv.at[h], -1, h)
        if h == 0:
            brecv[0] = bsend[0]

    for i, (f0, fn) in enumerate(FT):
        for q in range(2):
            gw2[f0 : f0 + fn, q * HALF : (q + 1) * HALF] = dot(
                hid[:, f0 : f0 + fn], xs[q, 1], TN
            ).astype(BF16)
    for q in range(2):
        for d0 in range(0, HALF, 256):
            gw1[q * HALF + d0 : q * HALF + d0 + 256, :] = dot(
                xs[q, 0, :, d0 : d0 + 256], gp[...], TN
            ).astype(BF16)

    total = jnp.zeros((1, TOK), F32)
    for h in range(CHUNKS):
        k0, kc = STARTS[h], SIZES[h]
        arrived(brecv, back_recv.at[h], h)
        stage_b[0 : kc * BACK_R] = brecv[pl.ds(k0, kc)].astype(F32).reshape(kc * BACK_R, 128)
        for s in range(CAP):
            rr = pl.ds(CAP * k0 + s * kc, kc)
            for j in range(LB):
                grows[rr, j * 128 : (j + 1) * 128] = stage_b[
                    pl.ds(s * LB + j, kc, stride=BACK_R), :
                ].astype(BF16)
            both = stage_b[pl.ds(CAP * LB + s, kc, stride=BACK_R), :]
            value = both[:, 0:1] + both[:, 64:65]
            total += jnp.sum(pick[rr, :].astype(F32) * value, axis=0, keepdims=True)
    ggate_ref[...] = total / gate

    for h in range(CHUNKS):
        arrived(sbuf, out_send.at[h], h)
        arrived(bsend, back_send.at[h], h)


def finish(gw1, gw2, pick, grows, ggate, gin_hbm, gate_out, gw1_hbm, gw2_hbm, gin, sem):
    copies = [
        pltpu.make_async_copy(gw1, gw1_hbm, sem.at[0]),
        pltpu.make_async_copy(gw2, gw2_hbm, sem.at[1]),
        pltpu.make_async_copy(gin, gin_hbm, sem.at[2]),
    ]
    copies[0].start()
    copies[1].start()
    gin[...] = dot(pick[...], grows[...], TN).astype(BF16)
    copies[2].start()
    gate_out[...] = ggate[...].reshape(TOK).astype(BF16)
    for copy in copies:
        copy.wait()


def body(tokens, cotangent, gate_prob, route_expert, route_slot, route_kept, w_in, w_out):
    vmem = pl.BlockSpec(memory_space=pltpu.VMEM)
    hbm = pl.BlockSpec(memory_space=pl.ANY)
    dma = pltpu.SemaphoreType.DMA
    work = pl.pallas_call(
        kernel,
        out_shape=(
            pltpu.VMEM((D, FF), BF16),
            pltpu.VMEM((FF, D), BF16),
            pltpu.VMEM((ROWS, TOK), BF16),
            pltpu.VMEM((ROWS, HALF), BF16),
            pltpu.VMEM((1, TOK), F32),
        ),
        in_specs=[hbm] * 8,
        out_specs=(vmem,) * 5,
        scratch_shapes=[
            pltpu.VMEM((TOK, HALF), BF16),
            pltpu.VMEM((TOK, HALF), BF16),
            pltpu.VMEM((TOK,), BF16),
            pltpu.VMEM((1, TOK), jnp.int32),
            pltpu.VMEM((1, TOK), jnp.int32),
            pltpu.VMEM((1, TOK), jnp.int32),
            pltpu.VMEM((2, HALF, FF), BF16),
            pltpu.VMEM((2, FF, HALF), BF16),
            pltpu.VMEM((BIG * OUT_R, 128), F32),
            pltpu.VMEM((BIG * BACK_R, 128), F32),
            pltpu.VMEM((PEERS, OUT_R, 128), BF16),
            pltpu.VMEM((PEERS, OUT_R, 128), BF16),
            pltpu.VMEM((2, 2, ROWS, HALF), BF16),
            pltpu.VMEM((ROWS, FF), BF16),
            pltpu.VMEM((ROWS, FF), BF16),
            pltpu.VMEM((BIG * CAP, FF), F32),
            pltpu.VMEM((BIG * CAP, FF), F32),
            pltpu.VMEM((ROWS, HALF + 128), F32),
            pltpu.VMEM((ROWS, HALF + 128), F32),
            pltpu.VMEM((PEERS, BACK_R, 128), BF16),
            pltpu.VMEM((PEERS, BACK_R, 128), BF16),
            dma((6,)),
            dma((4,)),
            dma((CHUNKS,)),
            dma((CHUNKS,)),
            dma((CHUNKS,)),
            dma((CHUNKS,)),
            dma((2 * CHUNKS,)),
            dma((2 * CHUNKS,)),
            pltpu.SemaphoreType.REGULAR,
        ],
        compiler_params=pltpu.CompilerParams(
            collective_id=0, has_side_effects=True, vmem_limit_bytes=40 << 20
        ),
    )(
        *(
            pltpu.with_memory_space_constraint(array, pltpu.HBM)
            for array in (
                tokens,
                cotangent,
                gate_prob,
                route_expert.reshape(1, TOK),
                route_slot.reshape(1, TOK),
                route_kept.reshape(1, TOK),
                w_in[0],
                w_out[0],
            )
        )
    )
    gin, ggate, gw1, gw2 = pl.pallas_call(
        finish,
        out_shape=(
            jax.ShapeDtypeStruct((TOK, HALF), BF16),
            jax.ShapeDtypeStruct((TOK,), BF16),
            jax.ShapeDtypeStruct((D, FF), BF16),
            jax.ShapeDtypeStruct((FF, D), BF16),
        ),
        in_specs=[hbm, hbm, vmem, vmem, vmem],
        out_specs=(hbm, vmem, hbm, hbm),
        scratch_shapes=[pltpu.VMEM((TOK, HALF), BF16), dma((3,))],
        compiler_params=pltpu.CompilerParams(vmem_limit_bytes=8 << 20),
    )(*work)
    return gin, ggate, gw1[None], gw2[None]


def solution(mesh):
    placed = (
        P(("gx", "gy"), "ta"),
        P(("gx", "gy"), "ta"),
        P(("gx", "gy")),
        P(("gx", "gy")),
        P(("gx", "gy")),
        P(("gx", "gy")),
        P(("gx", "gy"), None, "ta"),
        P(("gx", "gy"), "ta", None),
    )
    return jax.shard_map(
        body,
        mesh=mesh,
        in_specs=placed,
        out_specs=(
            P(("gx", "gy"), "ta"),
            P(("gx", "gy")),
            P(("gx", "gy"), None, "ta"),
            P(("gx", "gy"), "ta", None),
        ),
        check_vma=False,
    )
```

```python
import functools

import jax
import jax.numpy as jnp
from jax import lax
from jax.experimental import pallas as pl
from jax.experimental.pallas import tpu as pltpu
from jax.sharding import PartitionSpec as P

MESH = pl.DeviceIdType.MESH
F32 = jnp.float32
BF16 = jnp.bfloat16

tanh_scale = 0.7978845608
cubic_term = 0.044715

PEERS = 128
CAP = 3
SIZES = (64, 48, 16)
STARTS = tuple(sum(SIZES[:i]) for i in range(len(SIZES)))
CHUNKS = len(SIZES)
BIG = max(SIZES)
ROWS = PEERS * CAP
TOK = 256
ORDER = (4, 3, 5, 2, 6, 1, 7, 0)
D = 1024
HALF = 512
FF = 1408
LB = HALF // 128
OUT_R = 2 * CAP * LB
BACK_R = 16
FT = [(i, min(256, FF - i)) for i in range(0, FF, 256)]

NN = (((1,), (0,)), ((), ()))
NT = (((1,), (1,)), ((), ()))
TN = (((0,), (0,)), ((), ()))


def dot(a, b, dims):
    return lax.dot_general(a, b, dims, preferred_element_type=F32)


def coords():
    g = lax.axis_index("gy")
    return lax.axis_index("gx"), g // 4, g % 4, lax.axis_index("ta")


def await_bytes(ref, sem):
    pltpu.make_async_copy(ref, ref, sem).wait()


def kernel(
    tok_hbm, cot_hbm, gate_hbm, exp_hbm, slot_hbm, kept_hbm, w1_hbm, w2_hbm,
    gw1, gw2, pick, grows, ggate_ref,
    tok, cot, gate_ref, exp_ref, slot_ref, kept_ref, w1, w2, stage, stage_b, sbuf, rbuf, xs, hid, gp, pre_acc, up_acc,
    part_s, part_r, bsend, brecv,
    in_sem, w_sem, out_send, out_recv, back_send, back_recv, sib_send, sib_recv, plane_sem,
):
    z, x, y, c = coords()
    dzs = [lax.rem((1 - 2 * c) * d + 8, 8) for d in range(8)]
    zs = [lax.rem(z + d, 8) for d in range(8)]
    pairs = (
        (exp_hbm, exp_ref), (slot_hbm, slot_ref), (kept_hbm, kept_ref), (gate_hbm, gate_ref),
        (tok_hbm, tok), (cot_hbm, cot),
    )
    inputs = [pltpu.make_async_copy(src, dst, in_sem.at[i]) for i, (src, dst) in enumerate(pairs)]
    for copy in inputs:
        copy.start()
    weights = []
    for q in range(2):
        cols = pl.ds(q * HALF, HALF)
        weights.append(pltpu.make_async_copy(w1_hbm.at[cols], w1.at[q], w_sem.at[2 * q]))
        weights.append(pltpu.make_async_copy(w2_hbm.at[:, cols], w2.at[q], w_sem.at[2 * q + 1]))

    barrier = pltpu.get_barrier_semaphore()

    def ring(sem):
        for d in range(1, 8):
            pl.semaphore_signal(sem, 1, device_id={"gx": zs[d]}, device_id_type=MESH)

    xy = x * 4 + y
    for d in range(1, 16):
        pl.semaphore_signal(barrier, 1, device_id={"gy": lax.rem(xy + d, 16)}, device_id_type=MESH)
    ring(barrier)
    pl.semaphore_signal(barrier, 1, device_id={"ta": 1 - c}, device_id_type=MESH)
    for copy in weights:
        copy.start()
    for copy in inputs:
        copy.wait()

    expert = exp_ref[...]
    dz = ((expert >> 4) - z) & 7
    dx = (((expert >> 2) & 3) - x) & 3
    dy = ((expert & 3) - y) & 3
    k_tok = dy * 32 + dx * 8 + dz
    row_tok = CAP * STARTS[0] + slot_ref[...] * SIZES[0] + k_tok - STARTS[0]
    for k0, kc in zip(STARTS[1:], SIZES[1:]):
        row_tok = jnp.where(k_tok >= k0, CAP * k0 + slot_ref[...] * kc + k_tok - k0, row_tok)
    row_tok = jnp.where(kept_ref[...] == 1, row_tok, -1)
    gate = gate_ref[...].astype(F32).reshape(1, TOK)

    def build(h):
        k0, kc = STARTS[h], SIZES[h]
        rr = pl.ds(CAP * k0, CAP * kc)
        hot = lax.broadcasted_iota(jnp.int32, (CAP * kc, TOK), 0) + CAP * k0 == row_tok
        sel = jnp.where(hot, 1.0, 0.0).astype(BF16)
        pick[rr, :] = sel
        sel_gate = jnp.where(hot, gate, 0.0).astype(BF16)
        for a, (m, src) in enumerate(((sel, tok), (sel_gate, cot))):
            rows = dot(m, src[...], NN)
            for s in range(CAP):
                for j in range(LB):
                    stage[pl.ds((a * CAP + s) * LB + j, kc, stride=OUT_R), :] = rows[
                        s * kc : (s + 1) * kc, j * 128 : (j + 1) * 128
                    ]
        sbuf[pl.ds(k0, kc)] = stage[0 : kc * OUT_R].reshape(kc, OUT_R, 128).astype(BF16)

    def group(src, dst, ss, rs, sign, g, lo=0):
        gx_at = [lax.rem(z + sign * dzs[d] + 8, 8) for d in range(8)]
        gy_at = lax.rem(x + sign * (g % 4) + 4, 4) * 4 + lax.rem(y + sign * (g // 4) + 4, 4)
        for d in ORDER[: 8 - lo]:
            slot = g * 8 + dzs[d]
            pltpu.make_async_remote_copy(
                src_ref=src.at[slot], dst_ref=dst.at[slot], send_sem=ss, recv_sem=rs,
                device_id=(gx_at[d], gy_at, c), device_id_type=MESH,
            ).start()

    def exchange(src, dst, ss, rs, sign, h):
        def rest(g, carry):
            group(src, dst, ss, rs, sign, g)
            return carry

        lax.fori_loop(max(1, STARTS[h] // 8), (STARTS[h] + SIZES[h]) // 8, rest, 0)

    def arrived(ref, sem, h):
        lo = max(1, STARTS[h])
        await_bytes(ref.at[pl.ds(lo, STARTS[h] + SIZES[h] - lo)], sem)

    build(0)
    pl.semaphore_wait(barrier, 23)
    ring(plane_sem)
    group(sbuf, rbuf, out_send.at[0], out_recv.at[0], 1, 0, 1)
    pl.semaphore_wait(plane_sem, 7)
    exchange(sbuf, rbuf, out_send.at[0], out_recv.at[0], 1, 0)
    rbuf[0] = sbuf[0]
    for h in range(1, CHUNKS):
        build(h)
        exchange(sbuf, rbuf, out_send.at[h], out_recv.at[h], 1, h)

    stage_b[...] = jnp.zeros_like(stage_b)
    for copy in weights:
        copy.wait()

    def sibling(src, dst, sem):
        return pltpu.make_async_remote_copy(
            src_ref=src, dst_ref=dst, send_sem=sib_send.at[sem], recv_sem=sib_recv.at[sem],
            device_id={"ta": 1 - c}, device_id_type=MESH,
        )

    for h in range(CHUNKS):
        k0, kc = STARTS[h], SIZES[h]
        r0, rc = CAP * k0, CAP * kc
        rr = pl.ds(r0, rc)
        arrived(rbuf, out_recv.at[h], h)
        stage[0 : kc * OUT_R] = rbuf[pl.ds(k0, kc)].astype(F32).reshape(kc * OUT_R, 128)
        for a in range(2):
            for s in range(CAP):
                for j in range(LB):
                    xs[c, a, r0 + s * kc : r0 + (s + 1) * kc, j * 128 : (j + 1) * 128] = stage[
                        pl.ds((a * CAP + s) * LB + j, kc, stride=OUT_R), :
                    ].astype(BF16)
        share = sibling(xs.at[c, :, rr], xs.at[c, :, rr], 2 * h)
        share.start()
        for f0, fn in FT:
            pre_acc[0:rc, f0 : f0 + fn] = dot(xs[c, 0, rr], w1[c, :, f0 : f0 + fn], NN)
            up_acc[0:rc, f0 : f0 + fn] = dot(xs[c, 1, rr], w2[c, f0 : f0 + fn, :], NT)
        share.wait()

        gates = jnp.zeros((rc, 1), F32)
        for f0, fn in FT:
            pre = pre_acc[0:rc, f0 : f0 + fn] + dot(xs[1 - c, 0, rr], w1[1 - c, :, f0 : f0 + fn], NN)
            up = up_acc[0:rc, f0 : f0 + fn] + dot(xs[1 - c, 1, rr], w2[1 - c, f0 : f0 + fn, :], NT)
            sq = pre * pre
            th = jnp.tanh(tanh_scale * (pre + cubic_term * pre * sq))
            half = 0.5 * (1.0 + th)
            hb = (pre * half).astype(BF16)
            hid[rr, f0 : f0 + fn] = hb
            gates += jnp.sum(hb.astype(F32) * up, axis=1, keepdims=True)
            slope = half + 0.5 * pre * (1.0 - th * th) * tanh_scale * (1.0 + 3.0 * cubic_term * sq)
            gp[rr, f0 : f0 + fn] = (up * slope).astype(BF16)

        gates = jnp.broadcast_to(gates, (rc, 128))
        part_s[rr, 0:HALF] = dot(gp[rr, :], w1[1 - c], NT)
        part_s[rr, HALF : HALF + 128] = gates
        part = sibling(part_s.at[rr], part_r.at[rr], 2 * h + 1)
        part.start()
        own = dot(gp[rr, :], w1[c], NT)
        part.wait()
        own = own + part_r[rr, 0:HALF]
        gates = gates + part_r[rr, HALF : HALF + 128]
        high = gates.astype(BF16).astype(F32)
        gates = jnp.where(
            lax.broadcasted_iota(jnp.int32, (rc, 128), 1) < 64, high, gates - high
        )
        for s in range(CAP):
            for j in range(LB):
                stage_b[pl.ds(s * LB + j, kc, stride=BACK_R), :] = own[
                    s * kc : (s + 1) * kc, j * 128 : (j + 1) * 128
                ]
            stage_b[pl.ds(CAP * LB + s, kc, stride=BACK_R), :] = gates[s * kc : (s + 1) * kc]
        bsend[pl.ds(k0, kc)] = stage_b[0 : kc * BACK_R].reshape(kc, BACK_R, 128).astype(BF16)
        if h == 0:
            group(bsend, brecv, back_send.at[0], back_recv.at[0], -1, 0, 1)
        exchange(bsend, brecv, back_send.at[h], back_recv.at[h], -1, h)
        if h == 0:
            brecv[0] = bsend[0]

    for i, (f0, fn) in enumerate(FT):
        for q in range(2):
            gw2[f0 : f0 + fn, q * HALF : (q + 1) * HALF] = dot(
                hid[:, f0 : f0 + fn], xs[q, 1], TN
            ).astype(BF16)
    for q in range(2):
        for d0 in range(0, HALF, 256):
            gw1[q * HALF + d0 : q * HALF + d0 + 256, :] = dot(
                xs[q, 0, :, d0 : d0 + 256], gp[...], TN
            ).astype(BF16)

    total = jnp.zeros((1, TOK), F32)
    for h in range(CHUNKS):
        k0, kc = STARTS[h], SIZES[h]
        arrived(brecv, back_recv.at[h], h)
        stage_b[0 : kc * BACK_R] = brecv[pl.ds(k0, kc)].astype(F32).reshape(kc * BACK_R, 128)
        for s in range(CAP):
            rr = pl.ds(CAP * k0 + s * kc, kc)
            for j in range(LB):
                grows[rr, j * 128 : (j + 1) * 128] = stage_b[
                    pl.ds(s * LB + j, kc, stride=BACK_R), :
                ].astype(BF16)
            both = stage_b[pl.ds(CAP * LB + s, kc, stride=BACK_R), :]
            value = both[:, 0:1] + both[:, 64:65]
            total += jnp.sum(pick[rr, :].astype(F32) * value, axis=0, keepdims=True)
    ggate_ref[...] = total / gate

    for h in range(CHUNKS):
        arrived(sbuf, out_send.at[h], h)
        arrived(bsend, back_send.at[h], h)


def finish(gw1, gw2, pick, grows, ggate, gin_hbm, gate_out, gw1_hbm, gw2_hbm, gin, sem):
    copies = [
        pltpu.make_async_copy(gw1, gw1_hbm, sem.at[0]),
        pltpu.make_async_copy(gw2, gw2_hbm, sem.at[1]),
        pltpu.make_async_copy(gin, gin_hbm, sem.at[2]),
    ]
    copies[0].start()
    copies[1].start()
    gin[...] = dot(pick[...], grows[...], TN).astype(BF16)
    copies[2].start()
    gate_out[...] = ggate[...].reshape(TOK).astype(BF16)
    for copy in copies:
        copy.wait()


def body(tokens, cotangent, gate_prob, route_expert, route_slot, route_kept, w_in, w_out):
    vmem = pl.BlockSpec(memory_space=pltpu.VMEM)
    hbm = pl.BlockSpec(memory_space=pl.ANY)
    dma = pltpu.SemaphoreType.DMA
    work = pl.pallas_call(
        kernel,
        out_shape=(
            pltpu.VMEM((D, FF), BF16),
            pltpu.VMEM((FF, D), BF16),
            pltpu.VMEM((ROWS, TOK), BF16),
            pltpu.VMEM((ROWS, HALF), BF16),
            pltpu.VMEM((1, TOK), F32),
        ),
        in_specs=[hbm] * 8,
        out_specs=(vmem,) * 5,
        scratch_shapes=[
            pltpu.VMEM((TOK, HALF), BF16),
            pltpu.VMEM((TOK, HALF), BF16),
            pltpu.VMEM((TOK,), BF16),
            pltpu.VMEM((1, TOK), jnp.int32),
            pltpu.VMEM((1, TOK), jnp.int32),
            pltpu.VMEM((1, TOK), jnp.int32),
            pltpu.VMEM((2, HALF, FF), BF16),
            pltpu.VMEM((2, FF, HALF), BF16),
            pltpu.VMEM((BIG * OUT_R, 128), F32),
            pltpu.VMEM((BIG * BACK_R, 128), F32),
            pltpu.VMEM((PEERS, OUT_R, 128), BF16),
            pltpu.VMEM((PEERS, OUT_R, 128), BF16),
            pltpu.VMEM((2, 2, ROWS, HALF), BF16),
            pltpu.VMEM((ROWS, FF), BF16),
            pltpu.VMEM((ROWS, FF), BF16),
            pltpu.VMEM((BIG * CAP, FF), F32),
            pltpu.VMEM((BIG * CAP, FF), F32),
            pltpu.VMEM((ROWS, HALF + 128), F32),
            pltpu.VMEM((ROWS, HALF + 128), F32),
            pltpu.VMEM((PEERS, BACK_R, 128), BF16),
            pltpu.VMEM((PEERS, BACK_R, 128), BF16),
            dma((6,)),
            dma((4,)),
            dma((CHUNKS,)),
            dma((CHUNKS,)),
            dma((CHUNKS,)),
            dma((CHUNKS,)),
            dma((2 * CHUNKS,)),
            dma((2 * CHUNKS,)),
            pltpu.SemaphoreType.REGULAR,
        ],
        compiler_params=pltpu.CompilerParams(
            collective_id=0, has_side_effects=True, vmem_limit_bytes=40 << 20
        ),
    )(
        *(
            pltpu.with_memory_space_constraint(array, pltpu.HBM)
            for array in (
                tokens,
                cotangent,
                gate_prob,
                route_expert.reshape(1, TOK),
                route_slot.reshape(1, TOK),
                route_kept.reshape(1, TOK),
                w_in[0],
                w_out[0],
            )
        )
    )
    gin, ggate, gw1, gw2 = pl.pallas_call(
        finish,
        out_shape=(
            jax.ShapeDtypeStruct((TOK, HALF), BF16),
            jax.ShapeDtypeStruct((TOK,), BF16),
            jax.ShapeDtypeStruct((D, FF), BF16),
            jax.ShapeDtypeStruct((FF, D), BF16),
        ),
        in_specs=[hbm, hbm, vmem, vmem, vmem],
        out_specs=(hbm, vmem, hbm, hbm),
        scratch_shapes=[pltpu.VMEM((TOK, HALF), BF16), dma((3,))],
        compiler_params=pltpu.CompilerParams(vmem_limit_bytes=8 << 20),
    )(*work)
    return gin, ggate, gw1[None], gw2[None]


def solution(mesh):
    placed = (
        P(("gx", "gy"), "ta"),
        P(("gx", "gy"), "ta"),
        P(("gx", "gy")),
        P(("gx", "gy")),
        P(("gx", "gy")),
        P(("gx", "gy")),
        P(("gx", "gy"), None, "ta"),
        P(("gx", "gy"), "ta", None),
    )
    return jax.shard_map(
        body,
        mesh=mesh,
        in_specs=placed,
        out_specs=(
            P(("gx", "gy"), "ta"),
            P(("gx", "gy")),
            P(("gx", "gy"), None, "ta"),
            P(("gx", "gy"), "ta", None),
        ),
        check_vma=False,
    )
```

```python
import functools

import jax
import jax.numpy as jnp
from jax import lax
from jax.experimental import pallas as pl
from jax.experimental.pallas import tpu as pltpu
from jax.sharding import PartitionSpec as P

MESH = pl.DeviceIdType.MESH
F32 = jnp.float32
BF16 = jnp.bfloat16

tanh_scale = 0.7978845608
cubic_term = 0.044715

PEERS = 128
CAP = 3
SIZES = (64, 48, 16)
STARTS = tuple(sum(SIZES[:i]) for i in range(len(SIZES)))
CHUNKS = len(SIZES)
BIG = max(SIZES)
ROWS = PEERS * CAP
TOK = 256
ORDER = (4, 3, 5, 2, 6, 1, 7, 0)
D = 1024
HALF = 512
FF = 1408
LB = HALF // 128
OUT_R = 2 * CAP * LB
BACK_R = 16
FT = [(i, min(256, FF - i)) for i in range(0, FF, 256)]

NN = (((1,), (0,)), ((), ()))
NT = (((1,), (1,)), ((), ()))
TN = (((0,), (0,)), ((), ()))


def dot(a, b, dims):
    return lax.dot_general(a, b, dims, preferred_element_type=F32)


def coords():
    g = lax.axis_index("gy")
    return lax.axis_index("gx"), g // 4, g % 4, lax.axis_index("ta")


def await_bytes(ref, sem):
    pltpu.make_async_copy(ref, ref, sem).wait()


def kernel(
    tok_hbm, cot_hbm, gate_hbm, exp_hbm, slot_hbm, kept_hbm, w1_hbm, w2_hbm,
    gw1, gw2, pick, grows, ggate_ref,
    tok, cot, gate_ref, exp_ref, slot_ref, kept_ref, w1, w2, stage, stage_b, sbuf, rbuf, xs, hid, gp, pre_acc, up_acc,
    part_s, part_r, bsend, brecv,
    in_sem, w_sem, out_send, out_recv, back_send, back_recv, sib_send, sib_recv, plane_sem,
):
    z, x, y, c = coords()
    dzs = [lax.rem((1 - 2 * c) * d + 8, 8) for d in range(8)]
    zs = [lax.rem(z + d, 8) for d in range(8)]
    pairs = (
        (exp_hbm, exp_ref), (slot_hbm, slot_ref), (kept_hbm, kept_ref), (gate_hbm, gate_ref),
        (tok_hbm, tok), (cot_hbm, cot),
    )
    inputs = [pltpu.make_async_copy(src, dst, in_sem.at[i]) for i, (src, dst) in enumerate(pairs)]
    for copy in inputs:
        copy.start()
    weights = []
    for q in range(2):
        cols = pl.ds(q * HALF, HALF)
        weights.append(pltpu.make_async_copy(w1_hbm.at[cols], w1.at[q], w_sem.at[2 * q]))
        weights.append(pltpu.make_async_copy(w2_hbm.at[:, cols], w2.at[q], w_sem.at[2 * q + 1]))

    barrier = pltpu.get_barrier_semaphore()

    def ring(sem):
        for d in range(1, 8):
            pl.semaphore_signal(sem, 1, device_id={"gx": zs[d]}, device_id_type=MESH)

    xy = x * 4 + y
    for d in range(1, 16):
        pl.semaphore_signal(barrier, 1, device_id={"gy": lax.rem(xy + d, 16)}, device_id_type=MESH)
    ring(barrier)
    pl.semaphore_signal(barrier, 1, device_id={"ta": 1 - c}, device_id_type=MESH)
    for copy in weights:
        copy.start()
    for copy in inputs:
        copy.wait()

    expert = exp_ref[...]
    dz = ((expert >> 4) - z) & 7
    dx = (((expert >> 2) & 3) - x) & 3
    dy = ((expert & 3) - y) & 3
    k_tok = dy * 32 + dx * 8 + dz
    row_tok = CAP * STARTS[0] + slot_ref[...] * SIZES[0] + k_tok - STARTS[0]
    for k0, kc in zip(STARTS[1:], SIZES[1:]):
        row_tok = jnp.where(k_tok >= k0, CAP * k0 + slot_ref[...] * kc + k_tok - k0, row_tok)
    row_tok = jnp.where(kept_ref[...] == 1, row_tok, -1)
    gate = gate_ref[...].astype(F32).reshape(1, TOK)

    def build(h):
        k0, kc = STARTS[h], SIZES[h]
        rr = pl.ds(CAP * k0, CAP * kc)
        hot = lax.broadcasted_iota(jnp.int32, (CAP * kc, TOK), 0) + CAP * k0 == row_tok
        sel = jnp.where(hot, 1.0, 0.0).astype(BF16)
        pick[rr, :] = sel
        sel_gate = jnp.where(hot, gate, 0.0).astype(BF16)
        for a, (m, src) in enumerate(((sel, tok), (sel_gate, cot))):
            rows = dot(m, src[...], NN)
            for s in range(CAP):
                for j in range(LB):
                    stage[pl.ds((a * CAP + s) * LB + j, kc, stride=OUT_R), :] = rows[
                        s * kc : (s + 1) * kc, j * 128 : (j + 1) * 128
                    ]
        sbuf[pl.ds(k0, kc)] = stage[0 : kc * OUT_R].reshape(kc, OUT_R, 128).astype(BF16)

    def group(src, dst, ss, rs, sign, g, lo=0):
        gx_at = [lax.rem(z + sign * dzs[d] + 8, 8) for d in range(8)]
        gy_at = lax.rem(x + sign * (g % 4) + 4, 4) * 4 + lax.rem(y + sign * (g // 4) + 4, 4)
        for d in ORDER[: 8 - lo]:
            slot = g * 8 + dzs[d]
            pltpu.make_async_remote_copy(
                src_ref=src.at[slot], dst_ref=dst.at[slot], send_sem=ss, recv_sem=rs,
                device_id=(gx_at[d], gy_at, c), device_id_type=MESH,
            ).start()

    def exchange(src, dst, ss, rs, sign, h):
        def rest(g, carry):
            group(src, dst, ss, rs, sign, g)
            return carry

        lax.fori_loop(max(1, STARTS[h] // 8), (STARTS[h] + SIZES[h]) // 8, rest, 0)

    def arrived(ref, sem, h):
        lo = max(1, STARTS[h])
        await_bytes(ref.at[pl.ds(lo, STARTS[h] + SIZES[h] - lo)], sem)

    build(0)
    pl.semaphore_wait(barrier, 23)
    ring(plane_sem)
    group(sbuf, rbuf, out_send.at[0], out_recv.at[0], 1, 0, 1)
    pl.semaphore_wait(plane_sem, 7)
    exchange(sbuf, rbuf, out_send.at[0], out_recv.at[0], 1, 0)
    rbuf[0] = sbuf[0]
    for h in range(1, CHUNKS):
        build(h)
        exchange(sbuf, rbuf, out_send.at[h], out_recv.at[h], 1, h)

    stage_b[...] = jnp.zeros_like(stage_b)
    for copy in weights:
        copy.wait()

    def sibling(src, dst, sem):
        return pltpu.make_async_remote_copy(
            src_ref=src, dst_ref=dst, send_sem=sib_send.at[sem], recv_sem=sib_recv.at[sem],
            device_id={"ta": 1 - c}, device_id_type=MESH,
        )

    for h in range(CHUNKS):
        k0, kc = STARTS[h], SIZES[h]
        r0, rc = CAP * k0, CAP * kc
        rr = pl.ds(r0, rc)
        arrived(rbuf, out_recv.at[h], h)
        stage[0 : kc * OUT_R] = rbuf[pl.ds(k0, kc)].astype(F32).reshape(kc * OUT_R, 128)
        for a in range(2):
            for s in range(CAP):
                for j in range(LB):
                    xs[c, a, r0 + s * kc : r0 + (s + 1) * kc, j * 128 : (j + 1) * 128] = stage[
                        pl.ds((a * CAP + s) * LB + j, kc, stride=OUT_R), :
                    ].astype(BF16)
        share = sibling(xs.at[c, :, rr], xs.at[c, :, rr], 2 * h)
        share.start()
        for f0, fn in FT:
            pre_acc[0:rc, f0 : f0 + fn] = dot(xs[c, 0, rr], w1[c, :, f0 : f0 + fn], NN)
            up_acc[0:rc, f0 : f0 + fn] = dot(xs[c, 1, rr], w2[c, f0 : f0 + fn, :], NT)
        share.wait()

        gates = jnp.zeros((rc, 1), F32)
        for f0, fn in FT:
            pre = pre_acc[0:rc, f0 : f0 + fn] + dot(xs[1 - c, 0, rr], w1[1 - c, :, f0 : f0 + fn], NN)
            up = up_acc[0:rc, f0 : f0 + fn] + dot(xs[1 - c, 1, rr], w2[1 - c, f0 : f0 + fn, :], NT)
            sq = pre * pre
            th = jnp.tanh(tanh_scale * (pre + cubic_term * pre * sq))
            half = 0.5 * (1.0 + th)
            hb = (pre * half).astype(BF16)
            hid[rr, f0 : f0 + fn] = hb
            gates += jnp.sum(hb.astype(F32) * up, axis=1, keepdims=True)
            slope = half + 0.5 * pre * (1.0 - th * th) * tanh_scale * (1.0 + 3.0 * cubic_term * sq)
            gp[rr, f0 : f0 + fn] = (up * slope).astype(BF16)

        low_half = lax.broadcasted_iota(jnp.int32, (rc, 128), 1) < 64
        gates = jnp.broadcast_to(gates, (rc, 128))
        high = gates.astype(BF16).astype(F32)
        part_s[rr, 0:HALF] = dot(gp[rr, :], w1[1 - c], NT).astype(BF16)
        part_s[rr, HALF : HALF + 128] = jnp.where(low_half, high, gates - high).astype(BF16)
        part = sibling(part_s.at[rr], part_r.at[rr], 2 * h + 1)
        part.start()
        own = dot(gp[rr, :], w1[c], NT)
        part.wait()
        own = own + part_r[rr, 0:HALF].astype(F32)
        theirs = part_r[rr, HALF : HALF + 128].astype(F32)
        gates = gates + (theirs[:, 0:1] + theirs[:, 64:65])
        high = gates.astype(BF16).astype(F32)
        gates = jnp.where(low_half, high, gates - high)
        for s in range(CAP):
            for j in range(LB):
                stage_b[pl.ds(s * LB + j, kc, stride=BACK_R), :] = own[
                    s * kc : (s + 1) * kc, j * 128 : (j + 1) * 128
                ]
            stage_b[pl.ds(CAP * LB + s, kc, stride=BACK_R), :] = gates[s * kc : (s + 1) * kc]
        bsend[pl.ds(k0, kc)] = stage_b[0 : kc * BACK_R].reshape(kc, BACK_R, 128).astype(BF16)
        if h == 0:
            group(bsend, brecv, back_send.at[0], back_recv.at[0], -1, 0, 1)
        exchange(bsend, brecv, back_send.at[h], back_recv.at[h], -1, h)
        if h == 0:
            brecv[0] = bsend[0]

    for i, (f0, fn) in enumerate(FT):
        for q in range(2):
            gw2[f0 : f0 + fn, q * HALF : (q + 1) * HALF] = dot(
                hid[:, f0 : f0 + fn], xs[q, 1], TN
            ).astype(BF16)
    for q in range(2):
        for d0 in range(0, HALF, 256):
            gw1[q * HALF + d0 : q * HALF + d0 + 256, :] = dot(
                xs[q, 0, :, d0 : d0 + 256], gp[...], TN
            ).astype(BF16)

    total = jnp.zeros((1, TOK), F32)
    for h in range(CHUNKS):
        k0, kc = STARTS[h], SIZES[h]
        arrived(brecv, back_recv.at[h], h)
        stage_b[0 : kc * BACK_R] = brecv[pl.ds(k0, kc)].astype(F32).reshape(kc * BACK_R, 128)
        for s in range(CAP):
            rr = pl.ds(CAP * k0 + s * kc, kc)
            for j in range(LB):
                grows[rr, j * 128 : (j + 1) * 128] = stage_b[
                    pl.ds(s * LB + j, kc, stride=BACK_R), :
                ].astype(BF16)
            both = stage_b[pl.ds(CAP * LB + s, kc, stride=BACK_R), :]
            value = both[:, 0:1] + both[:, 64:65]
            total += jnp.sum(pick[rr, :].astype(F32) * value, axis=0, keepdims=True)
    ggate_ref[...] = total / gate

    for h in range(CHUNKS):
        arrived(sbuf, out_send.at[h], h)
        arrived(bsend, back_send.at[h], h)


def finish(gw1, gw2, pick, grows, ggate, gin_hbm, gate_out, gw1_hbm, gw2_hbm, gin, sem):
    copies = [
        pltpu.make_async_copy(gw1, gw1_hbm, sem.at[0]),
        pltpu.make_async_copy(gw2, gw2_hbm, sem.at[1]),
        pltpu.make_async_copy(gin, gin_hbm, sem.at[2]),
    ]
    copies[0].start()
    copies[1].start()
    gin[...] = dot(pick[...], grows[...], TN).astype(BF16)
    copies[2].start()
    gate_out[...] = ggate[...].reshape(TOK).astype(BF16)
    for copy in copies:
        copy.wait()


def body(tokens, cotangent, gate_prob, route_expert, route_slot, route_kept, w_in, w_out):
    vmem = pl.BlockSpec(memory_space=pltpu.VMEM)
    hbm = pl.BlockSpec(memory_space=pl.ANY)
    dma = pltpu.SemaphoreType.DMA
    work = pl.pallas_call(
        kernel,
        out_shape=(
            pltpu.VMEM((D, FF), BF16),
            pltpu.VMEM((FF, D), BF16),
            pltpu.VMEM((ROWS, TOK), BF16),
            pltpu.VMEM((ROWS, HALF), BF16),
            pltpu.VMEM((1, TOK), F32),
        ),
        in_specs=[hbm] * 8,
        out_specs=(vmem,) * 5,
        scratch_shapes=[
            pltpu.VMEM((TOK, HALF), BF16),
            pltpu.VMEM((TOK, HALF), BF16),
            pltpu.VMEM((TOK,), BF16),
            pltpu.VMEM((1, TOK), jnp.int32),
            pltpu.VMEM((1, TOK), jnp.int32),
            pltpu.VMEM((1, TOK), jnp.int32),
            pltpu.VMEM((2, HALF, FF), BF16),
            pltpu.VMEM((2, FF, HALF), BF16),
            pltpu.VMEM((BIG * OUT_R, 128), F32),
            pltpu.VMEM((BIG * BACK_R, 128), F32),
            pltpu.VMEM((PEERS, OUT_R, 128), BF16),
            pltpu.VMEM((PEERS, OUT_R, 128), BF16),
            pltpu.VMEM((2, 2, ROWS, HALF), BF16),
            pltpu.VMEM((ROWS, FF), BF16),
            pltpu.VMEM((ROWS, FF), BF16),
            pltpu.VMEM((BIG * CAP, FF), F32),
            pltpu.VMEM((BIG * CAP, FF), F32),
            pltpu.VMEM((ROWS, HALF + 128), BF16),
            pltpu.VMEM((ROWS, HALF + 128), BF16),
            pltpu.VMEM((PEERS, BACK_R, 128), BF16),
            pltpu.VMEM((PEERS, BACK_R, 128), BF16),
            dma((6,)),
            dma((4,)),
            dma((CHUNKS,)),
            dma((CHUNKS,)),
            dma((CHUNKS,)),
            dma((CHUNKS,)),
            dma((2 * CHUNKS,)),
            dma((2 * CHUNKS,)),
            pltpu.SemaphoreType.REGULAR,
        ],
        compiler_params=pltpu.CompilerParams(
            collective_id=0, has_side_effects=True, vmem_limit_bytes=40 << 20
        ),
    )(
        *(
            pltpu.with_memory_space_constraint(array, pltpu.HBM)
            for array in (
                tokens,
                cotangent,
                gate_prob,
                route_expert.reshape(1, TOK),
                route_slot.reshape(1, TOK),
                route_kept.reshape(1, TOK),
                w_in[0],
                w_out[0],
            )
        )
    )
    gin, ggate, gw1, gw2 = pl.pallas_call(
        finish,
        out_shape=(
            jax.ShapeDtypeStruct((TOK, HALF), BF16),
            jax.ShapeDtypeStruct((TOK,), BF16),
            jax.ShapeDtypeStruct((D, FF), BF16),
            jax.ShapeDtypeStruct((FF, D), BF16),
        ),
        in_specs=[hbm, hbm, vmem, vmem, vmem],
        out_specs=(hbm, vmem, hbm, hbm),
        scratch_shapes=[pltpu.VMEM((TOK, HALF), BF16), dma((3,))],
        compiler_params=pltpu.CompilerParams(vmem_limit_bytes=8 << 20),
    )(*work)
    return gin, ggate, gw1[None], gw2[None]


def solution(mesh):
    placed = (
        P(("gx", "gy"), "ta"),
        P(("gx", "gy"), "ta"),
        P(("gx", "gy")),
        P(("gx", "gy")),
        P(("gx", "gy")),
        P(("gx", "gy")),
        P(("gx", "gy"), None, "ta"),
        P(("gx", "gy"), "ta", None),
    )
    return jax.shard_map(
        body,
        mesh=mesh,
        in_specs=placed,
        out_specs=(
            P(("gx", "gy"), "ta"),
            P(("gx", "gy")),
            P(("gx", "gy"), None, "ta"),
            P(("gx", "gy"), "ta", None),
        ),
        check_vma=False,
    )
```
